256 devices in a mesh: gx: 8 (over z), gy: 8 (over x, core), gz: 4 (over y).
Axes of the slice: x: 4, y: 4, z: 8, core: 2. Of those that a mesh axis runs over, the one named last changes fastest.
Arguments:
- thermal_state: float32 [32, 256, 1024], P('gz', 'gy', 'gx'), may hold values from -6 to 6
- diffusion_ratio: float32 [32, 256, 1024], P('gz', 'gy', 'gx'), may hold values from 100 to 100000
Outputs:
- advanced: float32 [32, 256, 1024], P('gz', 'gy', 'gx')
The draws below stay inside these ranges and needn't reach their ends.
All inputs are finite; a program needn't handle non-finite values.
Results may differ from the reference program's by a relative error of at most 0.0028.
Values sent between devices are 32-bit elements; how exact they have to be, the bound alone decides.
A program may use at most 64 MiB of HBM per device.

```python
import math
import jax
import jax.numpy as jnp
from jax import lax

GRID_WIDTH_EAST = 1024
GRID_WIDTH_NORTH = 256
GRID_WIDTH_DEPTH = 32


def shard_levels(own_key, shape, split, least, largest):
    def one(axis_at, parts):
        heights = jax.random.uniform(jax.random.fold_in(jax.random.fold_in(own_key, 6), axis_at), (parts,), jnp.float32, least / len(split), largest / len(split))
        return jnp.repeat(jnp.exp(heights), shape[axis_at] // parts).reshape((-1,) + (1,) * (len(shape) - axis_at - 1))

    factor_of = one(*split[0])
    for cut in split[1:]:
        factor_of = factor_of * one(*cut)
    return factor_of


def centred(stream_key, shape, spread, reach, shards=(), kind=jnp.bfloat16):
    level = shard_levels(stream_key, shape, shards, -0.22, 0.18) if shards else 1.0
    array = jax.random.normal(stream_key, shape, jnp.float32) * spread * level
    return jnp.minimum(jnp.maximum(array, -reach), reach).astype(kind)


def setup_inputs(seed: int = 0) -> dict:
    splits = jax.random.split(jax.random.key(seed), 3)
    thermal_state = centred(splits[0], (GRID_WIDTH_DEPTH, GRID_WIDTH_NORTH, GRID_WIDTH_EAST), 1.0, 6.0, ((0, 4), (1, 8), (2, 8)), jnp.float32)
    diffusion_ratio = jnp.clip(jnp.exp(math.log(100000.0) - 6.9077553 * jax.random.uniform(splits[1], (GRID_WIDTH_DEPTH, GRID_WIDTH_NORTH, GRID_WIDTH_EAST), jnp.float32) ** shard_levels(splits[1], (GRID_WIDTH_DEPTH, GRID_WIDTH_NORTH, GRID_WIDTH_EAST), ((0, 4), (1, 8), (2, 8)), -0.2, 0.2)), 100.0, 100000.0)
    return dict(thermal_state=thermal_state, diffusion_ratio=diffusion_ratio)


def face_terms(diffusion_ratio, axis_dim):
    length = diffusion_ratio.shape[axis_dim]
    first_part = lax.slice_in_dim(diffusion_ratio, 0, length - 1, axis=axis_dim)
    second_part = lax.slice_in_dim(diffusion_ratio, 1, length, axis=axis_dim)
    inner_faces = 2.0 * first_part * second_part / (first_part + second_part)
    low_wall = 2.0 * lax.slice_in_dim(diffusion_ratio, 0, 1, axis=axis_dim)
    high_wall = 2.0 * lax.slice_in_dim(diffusion_ratio, length - 1, length, axis=axis_dim)
    h_low = jnp.concatenate([low_wall, inner_faces], axis=axis_dim)
    h_high = jnp.concatenate([inner_faces, high_wall], axis=axis_dim)
    return h_low, h_high


def second_difference_row(field, h_low, h_high, axis_dim):
    length = field.shape[axis_dim]
    zero_plane = jnp.zeros_like(lax.slice_in_dim(field, 0, 1, axis=axis_dim))
    before = jnp.concatenate([zero_plane, lax.slice_in_dim(field, 0, length - 1, axis=axis_dim)], axis=axis_dim)
    after = jnp.concatenate([lax.slice_in_dim(field, 1, length, axis=axis_dim), zero_plane], axis=axis_dim)
    return h_low * (before - field) + h_high * (after - field)


def tridiagonal(lower_band, middle, upper_band, right_side):
    def forward(carry, row_data):
        coef_prev, value_prev = carry
        low_entry, mid_entry, up_entry, side_entry = row_data
        denom = mid_entry - low_entry * coef_prev
        coef_new = up_entry / denom
        value_new = (side_entry - low_entry * value_prev) / denom
        return (coef_new, value_new), (coef_new, value_new)

    zero_row = jnp.zeros_like(right_side[0])
    _, (coefs, values) = lax.scan(forward, (zero_row, zero_row), (lower_band, middle, upper_band, right_side))

    def backward(next_value, row_data):
        coef_entry, value_entry = row_data
        result = value_entry - coef_entry * next_value
        return result, result

    _, solution = lax.scan(backward, zero_row, (coefs, values), reverse=True)
    return solution


def solve_along(right_side, h_low, h_high, axis_dim):
    length = right_side.shape[axis_dim]
    position = lax.broadcasted_iota(jnp.int32, right_side.shape, axis_dim)
    lower_band = jnp.where(position == 0, 0.0, -0.5 * h_low).astype(right_side.dtype)
    upper_band = jnp.where(position == length - 1, 0.0, -0.5 * h_high).astype(right_side.dtype)
    middle = 1.0 + 0.5 * (h_low + h_high)
    moved = [jnp.moveaxis(item, axis_dim, 0) for item in (lower_band, middle, upper_band, right_side)]
    return jnp.moveaxis(tridiagonal(*moved), 0, axis_dim)


def reference(thermal_state, diffusion_ratio):
    western_adjacent, eastern_adjacent = face_terms(diffusion_ratio, 2)
    southern_adjacent, northern_adjacent = face_terms(diffusion_ratio, 1)
    bottom_adjacent, top_adjacent = face_terms(diffusion_ratio, 0)
    curvature_east = second_difference_row(thermal_state, western_adjacent, eastern_adjacent, 2)
    curvature_north = second_difference_row(thermal_state, southern_adjacent, northern_adjacent, 1)
    curvature_depth = second_difference_row(thermal_state, bottom_adjacent, top_adjacent, 0)
    explicit_forcing = thermal_state + 0.5 * curvature_east + curvature_north + curvature_depth
    section_x = solve_along(explicit_forcing, western_adjacent, eastern_adjacent, 2)
    section_y = solve_along(section_x - 0.5 * curvature_north, southern_adjacent, northern_adjacent, 1)
    return solve_along(section_y - 0.5 * curvature_depth, bottom_adjacent, top_adjacent, 0)
```

```python
import functools

import jax
import jax.numpy as jnp
from jax import lax
from jax.experimental import pallas as pl
from jax.experimental.pallas import tpu as pltpu
from jax.sharding import PartitionSpec as P

MESH = pl.DeviceIdType.MESH
NZ, NY, NX = 8, 32, 128
GROUP = 4


def rcp(x):
    return 1.0 / x


def edge(a, b):
    return a * b * rcp(a + b)


def lane_roll(x, by):
    return pltpu.roll(x, by % NX, x.ndim - 1)


class Gather:
    def __init__(self, axis, count, buf, send, recv):
        self.axis, self.count, self.buf, self.send, self.recv = axis, count, buf, send, recv
        self.me = lax.axis_index(axis)

    def copy(self, slot, peer, step):
        return pltpu.make_async_remote_copy(
            src_ref=self.buf.at[slot],
            dst_ref=self.buf.at[slot],
            send_sem=self.send.at[step - 1],
            recv_sem=self.recv.at[slot],
            device_id={self.axis: peer},
            device_id_type=MESH,
        )

    def start(self):
        for step in range(1, self.count):
            self.copy(self.me, lax.rem(self.me + step, self.count), step).start()

    def wait_recv(self):
        for step in range(1, self.count):
            peer = lax.rem(self.me + step, self.count)
            self.copy(peer, peer, step).wait_recv()

    def wait_send(self):
        for step in range(1, self.count):
            self.copy(self.me, lax.rem(self.me + step, self.count), step).wait_send()


class Halo:
    def __init__(self, axis, count, low, high, buf, send, recv):
        self.axis, self.count, self.buf, self.send, self.recv = axis, count, buf, send, recv
        self.me = lax.axis_index(axis)
        self.ends = (high, low)

    def copy(self, side):
        step = (1, self.count - 1)[side]
        return pltpu.make_async_remote_copy(
            src_ref=self.ends[side],
            dst_ref=self.buf.at[side],
            send_sem=self.send.at[side],
            recv_sem=self.recv.at[side],
            device_id={self.axis: lax.rem(self.me + step, self.count)},
            device_id_type=MESH,
        )

    def start(self):
        for side in range(2):
            self.copy(side).start()

    def wait_recv(self):
        for side in range(2):
            self.copy(side).wait_recv()

    def wait_send(self):
        for side in range(2):
            self.copy(side).wait_send()


def chain_matrix(edges, store_rho, store_inv, store_p, store_q):
    last = len(edges)
    looking = edges[last - 1]
    rhos = [None] * last
    for i in range(last - 2, -1, -1):
        inv = rcp(edges[i] + (1.0 + looking))
        rhos[i] = edges[i] * inv
        store_rho(i, rhos[i])
        store_inv(i, inv)
        looking = rhos[i] * (1.0 + looking)
    looking = edges[0]
    lambdas = [None] * (last + 1)
    for i in range(2, last + 1):
        lambdas[i] = edges[i - 1] * rcp(edges[i - 1] + (1.0 + looking))
        looking = lambdas[i] * (1.0 + looking)
    one = jnp.ones_like(edges[0])
    zero = jnp.zeros_like(one)
    store_p(0, one)
    store_p(last, zero)
    store_q(0, zero)
    store_q(last, one)
    resp, ground_first = one, one
    for i in range(last - 1):
        resp = rhos[i] * resp
        store_p(i + 1, resp)
        ground_first = ground_first + resp
    resp, ground_last = one, one
    for i in range(last, 1, -1):
        resp = lambdas[i] * resp
        store_q(i - 1, resp)
        ground_last = ground_last + resp
    return ground_first, ground_last, edges[0] * resp


def chain_base(length, side, rho, inv, store):
    sums = [None] * length
    total = side(length - 2)
    sums[length - 2] = total
    for i in range(length - 3, 0, -1):
        total = side(i) + rho(i) * total
        sums[i] = total
    value = inv(0) * sums[1]
    store(1, value)
    for i in range(1, length - 2):
        value = rho(i) * value + inv(i) * sums[i + 1]
        store(i + 1, value)


def device_chain(count, me, ground_first, ground_last, inner, face):
    up_inner, up_face, gf = [None] * count, [None] * (count + 1), [None] * count
    gf[0] = ground_first[0]
    for q in range(count):
        up_inner[q] = inner[q] * rcp(inner[q] + gf[q])
        if q < count - 1:
            behind = ground_last[q] + up_inner[q] * gf[q]
            up_face[q + 1] = face[q + 1] * rcp(face[q + 1] + behind)
            gf[q + 1] = ground_first[q + 1] + up_face[q + 1] * behind
    down_inner, down_face, gl = [None] * count, [None] * (count + 1), [None] * count
    gl[count - 1] = ground_last[count - 1]
    for q in range(count - 1, -1, -1):
        down_inner[q] = inner[q] * rcp(inner[q] + gl[q])
        if q > 0:
            behind = ground_first[q] + down_inner[q] * gl[q]
            down_face[q] = face[q] * rcp(face[q] + behind)
            gl[q - 1] = ground_last[q - 1] + down_face[q] * behind
    zero = jnp.zeros_like(gf[0])

    def own(values):
        out = zero
        for q in range(count):
            if values[q] is not None:
                out = jnp.where(me == q, values[q], out)
        return out

    own_f, own_l, own_i = own(gf), own(gl), own(inner)
    scale = rcp(own_f * (own_l + own_i) + own_i * own_l)
    aa, bb, cc = (own_l + own_i) * scale, (own_f + own_i) * scale, own_i * scale
    from_low_f, from_low_l = [zero] * count, [zero] * count
    via_low = [zero] * count
    carry = zero
    for q in range(count - 2, -1, -1):
        via_low[q] = jnp.where(me == q + 1, 1.0, carry)
        from_low_l[q] = via_low[q] * up_face[q + 1]
        from_low_f[q] = from_low_l[q] * up_inner[q]
        carry = from_low_f[q]
    from_high_f, from_high_l = [zero] * count, [zero] * count
    via_high = [zero] * count
    carry = zero
    for q in range(1, count):
        via_high[q] = jnp.where(me == q - 1, 1.0, carry)
        from_high_f[q] = via_high[q] * down_face[q]
        from_high_l[q] = from_high_f[q] * down_inner[q]
        carry = from_high_l[q]
    return dict(
        aa=aa, bb=bb, cc=cc,
        low_f=from_low_f, low_l=from_low_l, high_f=from_high_f, high_l=from_high_l,
        via_low=via_low, via_high=via_high,
        up_inner=own(up_inner), up_face=own(up_face[1:]), down_inner=own(down_inner), down_face=own(down_face[:count]),
    )


def kernel(counts, t_hbm, c_hbm, out_ref, s):
    nx, ny, nz = counts
    mx, my, mz = lax.axis_index("gx"), lax.axis_index("gy"), lax.axis_index("gz")
    lane = lax.broadcasted_iota(jnp.int32, (NZ, NX), 1)

    barrier = pltpu.get_barrier_semaphore()
    for axis, me, count in (("gz", mz, nz), ("gy", my, ny), ("gx", mx, nx)):
        for step in range(1, count):
            pl.semaphore_signal(
                barrier, inc=1, device_id={axis: lax.rem(me + step, count)}, device_id_type=MESH
            )
    load_t = pltpu.make_async_copy(t_hbm, s["tc"].at[0], s["load"].at[0])
    load_c = pltpu.make_async_copy(c_hbm, s["tc"].at[1], s["load"].at[1])
    load_t.start()
    load_c.start()

    tc = s["tc"]
    halo_z = Halo("gz", nz, tc.at[:, pl.ds(0, NY)], tc.at[:, pl.ds((NZ - 1) * NY, NY)], s["hz"], s["hz_s"], s["hz_r"])
    halo_y = Halo("gy", ny, s["ey"].at[0], s["ey"].at[1], s["hy"], s["hy_s"], s["hy_r"])
    info_x = Gather("gx", nx, s["ix"], s["ix_s"], s["ix_r"])
    info_y = Gather("gy", ny, s["iy"], s["iy_s"], s["iy_r"])
    info_z = Gather("gz", nz, s["iz"], s["iz_s"], s["iz_r"])
    side_x = Gather("gx", nx, s["bx"], s["bx_s"], s["bx_r"])
    side_y = Gather("gy", ny, s["by"], s["by_s"], s["by_r"])
    side_z = Gather("gz", nz, s["bz"], s["bz_s"], s["bz_r"])

    load_t.wait()
    load_c.wait()
    for side, y in ((0, 0), (1, NY - 1)):
        for k in range(2):
            s["ey"][side, k] = tc[k, pl.ds(y, NZ, stride=NY), :]
    pl.semaphore_wait(barrier, nx + ny + nz - 3)
    halo_y.start()
    halo_z.start()

    info_a, info_b = jnp.zeros((NZ, NX), jnp.float32), jnp.zeros((NZ, NX), jnp.float32)
    for y0 in range(0, NY, GROUP):
        rows = pl.ds(y0, GROUP)
        t = jnp.stack([tc[0, pl.ds(y, NZ, stride=NY), :] for y in range(y0, y0 + GROUP)])
        c = jnp.stack([tc[1, pl.ds(y, NZ, stride=NY), :] for y in range(y0, y0 + GROUP)])
        s["ty"][rows] = t
        s["cy"][rows] = c
        spot = lax.broadcasted_iota(jnp.int32, t.shape, 2)
        e_high = edge(c, lane_roll(c, -1))
        e_low = lane_roll(e_high, 1)
        flux = jnp.where(spot == NX - 1, 0.0, 2.0 * e_high * (lane_roll(t, -1) - t))
        s["fx"][rows] = t + 0.5 * (flux - lane_roll(flux, 1))
        inv = rcp(1.0 + e_low + e_high)
        is_first, is_last = spot == 0, spot == NX - 1
        gnd = jnp.where(is_first | is_last, 0.0, inv)
        low = jnp.where(is_first, 1.0, jnp.where(is_last, 0.0, e_low * inv))
        high = jnp.where(is_last, 1.0, jnp.where(is_first, 0.0, e_high * inv))
        s["x_inv"][rows] = gnd
        for level in range(7):
            k = 1 << level
            no_low, no_high = spot < k, spot >= NX - k
            gnd_m = jnp.where(no_low, 0.0, lane_roll(gnd, k))
            low_m = jnp.where(no_low, 1.0, lane_roll(low, k))
            gnd_p = jnp.where(no_high, 0.0, lane_roll(gnd, -k))
            high_p = jnp.where(no_high, 1.0, lane_roll(high, -k))
            keep = rcp(gnd + low * (gnd_m + low_m) + high * (gnd_p + high_p))
            take_low, take_high = low * keep, high * keep
            s["x_keep"][level, rows] = keep
            s["x_low"][level, rows] = jnp.where(no_low, 0.0, take_low)
            s["x_high"][level, rows] = jnp.where(no_high, 0.0, take_high)
            gnd = gnd * keep + take_low * gnd_m + take_high * gnd_p
            low = take_low * low_m
            high = take_high * high_p
        s["x_p"][rows] = low
        s["x_q"][rows] = high
        ground = jnp.where(spot == 1, e_low, e_high) * gnd
        joint = e_low * high
        for j in range(GROUP):
            y = y0 + j
            for at, value, source in ((0, t, 0), (32, t, NX - 1), (64, c, 0), (96, c, NX - 1)):
                info_a = jnp.where(lane == at + y, lane_roll(value[j], at + y - source), info_a)
            for at, value, source in ((0, ground, 1), (32, ground, NX - 2), (64, joint, 1)):
                info_b = jnp.where(lane == at + y, lane_roll(value[j], at + y - source), info_b)
    s["ix"][mx, 0] = info_a
    s["ix"][mx, 1] = info_b + jnp.where(lane < 64, 1.0, 0.0)
    info_x.start()

    tz = [tc[0, pl.ds(z * NY, NY), :] for z in range(NZ)]
    cz = [tc[1, pl.ds(z * NY, NY), :] for z in range(NZ)]
    edges_z = [edge(cz[z], cz[z + 1]) for z in range(NZ - 1)]
    flux_z = [2.0 * edges_z[z] * (tz[z + 1] - tz[z]) for z in range(NZ - 1)]
    for z in range(NZ):
        lap = (flux_z[z] if z < NZ - 1 else 0.0) - (flux_z[z - 1] if z > 0 else 0.0)
        s["lz"][z] = lap
        if z < NZ - 1:
            s["ez"][z] = edges_z[z]
        if 0 < z < NZ - 1:
            for tile in range(NY // 8):
                s["lzy"][pl.ds(tile * 64 + z, 8, stride=8), :] = lap[tile * 8:tile * 8 + 8]
    below = None
    for y in range(NY):
        lap = 0.0
        if y < NY - 1:
            e = edge(s["cy"][y], s["cy"][y + 1])
            s["eyy"][y] = e
            above = 2.0 * e * (s["ty"][y + 1] - s["ty"][y])
            lap = above
        if y > 0:
            lap = lap - below
        below = above
        s["ly"][y] = lap

    halo_y.wait_recv()
    halo_z.wait_recv()
    wall_y, wall_z = [], []
    for side, me, count in ((0, my, ny), (1, my, ny)):
        at_wall = me == (0, count - 1)[side]
        y = (0, NY - 1)[side]
        t_end, c_end = s["ty"][y], s["cy"][y]
        face = jnp.where(at_wall, c_end, edge(s["hy"][side, 1], c_end))
        beyond = jnp.where(at_wall, 0.0, s["hy"][side, 0])
        s["ly"][y] = s["ly"][y] + 2.0 * face * (beyond - t_end)
        wall_y.append((at_wall, face))
    for side in range(2):
        at_wall = mz == (0, nz - 1)[side]
        z = (0, NZ - 1)[side]
        t_end, c_end = tc[0, pl.ds(z * NY, NY), :], tc[1, pl.ds(z * NY, NY), :]
        face = jnp.where(at_wall, c_end, edge(s["hz"][side, 1], c_end))
        beyond = jnp.where(at_wall, 0.0, s["hz"][side, 0])
        lap = s["lz"][z] + 2.0 * face * (beyond - t_end)
        s["lz"][z] = lap
        for tile in range(NY // 8):
            s["lzy"][pl.ds(tile * 64 + z, 8, stride=8), :] = lap[tile * 8:tile * 8 + 8]
        wall_z.append((at_wall, face))

    packed = jnp.zeros((NZ, NX), jnp.float32)
    for y in range(NY):
        f = s["fx"][y] + s["ly"][y] + s["lzy"][pl.ds(y * 8, 8), :]
        s["fx"][y] = f
        first = jnp.sum(s["x_p"][y] * f, axis=1, keepdims=True)
        final = jnp.sum(s["x_q"][y] * f, axis=1, keepdims=True)
        packed = jnp.where(lane == y, first, jnp.where(lane == 32 + y, final, packed))
    s["bx"][mx] = packed
    side_x.start()

    edges_y = [s["eyy"][y] for y in range(NY - 1)]

    def put(name):
        def store(i, value):
            s[name][i] = value
        return store

    g_first, g_last, joint = chain_matrix(edges_y, put("y_rho"), put("y_inv"), put("y_p"), put("y_q"))
    (wall_low, face_low), (wall_high, face_high) = wall_y
    s["iy"][my, 0] = g_first + jnp.where(wall_low, face_low, 0.0)
    s["iy"][my, 1] = g_last + jnp.where(wall_high, face_high, 0.0)
    s["iy"][my, 2] = joint
    s["iy"][my, 3] = face_low
    info_y.start()
    g_first, g_last, joint = chain_matrix(
        [s["ez"][z] for z in range(NZ - 1)], put("z_rho"), put("z_inv"), put("z_p"), put("z_q")
    )
    (wall_low, face_low), (wall_high, face_high) = wall_z
    s["iz"][mz, 0] = g_first + jnp.where(wall_low, face_low, 0.0)
    s["iz"][mz, 1] = g_last + jnp.where(wall_high, face_high, 0.0)
    s["iz"][mz, 2] = joint
    s["iz"][mz, 3] = face_low
    info_z.start()

    for y0 in range(0, NY, GROUP):
        rows = pl.ds(y0, GROUP)
        f = s["fx"][rows] * s["x_inv"][rows]
        for level in range(7):
            k = 1 << level
            f = (
                s["x_keep"][level, rows] * f
                + s["x_low"][level, rows] * lane_roll(f, k)
                + s["x_high"][level, rows] * lane_roll(f, -k)
            )
        s["fx"][rows] = f

    info_x.wait_recv()
    parts = []
    for q in range(nx):
        a, b = s["ix"][q, 0], s["ix"][q, 1]
        parts.append([a, lane_roll(a, -32), lane_roll(a, -64), lane_roll(a, -96), b, lane_roll(b, -32), lane_roll(b, -64)])
    faces = [None] * nx
    add_f, add_l = [None] * nx, [None] * nx
    gf, gl = [p[4] for p in parts], [p[5] for p in parts]
    add_f[0] = -parts[0][2] * parts[0][0]
    gf[0] = gf[0] + parts[0][2]
    add_l[nx - 1] = -parts[nx - 1][3] * parts[nx - 1][1]
    gl[nx - 1] = gl[nx - 1] + parts[nx - 1][3]
    for q in range(1, nx):
        faces[q] = edge(parts[q - 1][3], parts[q][2])
        flow = faces[q] * (parts[q][0] - parts[q - 1][1])
        add_f[q] = -flow
        add_l[q - 1] = flow
    ch = device_chain(nx, mx, gf, gl, [p[6] for p in parts], faces)
    const_f, const_l = 0.0, 0.0
    for q in range(nx):
        here = jnp.where(mx == q, 1.0, 0.0)
        lf, ll = ch["low_f"][q] + here, ch["low_l"][q]
        hf, hl = ch["high_f"][q], ch["high_l"][q] + here
        ff, fl = ch["aa"] * lf + ch["cc"] * hf, ch["aa"] * ll + ch["cc"] * hl
        lf, ll = ch["cc"] * lf + ch["bb"] * hf, ch["cc"] * ll + ch["bb"] * hl
        const_f = const_f + ff * add_f[q] + fl * add_l[q]
        const_l = const_l + lf * add_f[q] + ll * add_l[q]
        s["wx"][q, 0] = jnp.where(lane < 32, ff, lane_roll(fl, 32))
        s["wx"][q, 1] = jnp.where(lane < 32, lf, lane_roll(ll, 32))
    side_x.wait_recv()
    first, final = 0.0, 0.0
    for q in range(nx):
        b = jnp.where(lane < 64, s["bx"][q], 0.0)
        first = first + jnp.where(lane < 64, s["wx"][q, 0], 0.0) * b
        final = final + jnp.where(lane < 64, s["wx"][q, 1], 0.0) * b
    first = first + lane_roll(first, -32) + const_f
    final = final + lane_roll(final, -32) + const_l

    sum_first, sum_last = 0.0, 0.0
    for y in range(NY):
        u = (
            s["fx"][y]
            + s["x_p"][y] * jnp.broadcast_to(first[:, y:y + 1], (NZ, NX))
            + s["x_q"][y] * jnp.broadcast_to(final[:, y:y + 1], (NZ, NX))
        )
        f = u - 0.5 * s["ly"][y]
        s["fy"][y] = f
        sum_first = sum_first + s["y_p"][y] * f
        sum_last = sum_last + s["y_q"][y] * f

    def reduced_weights(info, buf, count, me):
        info.wait_recv()
        ch = device_chain(
            count, me, *[[buf[q, k] for q in range(count)] for k in range(4)]
        )
        to_f = [ch["aa"] * ch["via_low"][q] + ch["cc"] * ch["via_high"][q] for q in range(count)]
        to_l = [ch["cc"] * ch["via_low"][q] + ch["bb"] * ch["via_high"][q] for q in range(count)]
        return ch, to_f, to_l

    ch, to_f, to_l = reduced_weights(info_y, s["iy"], ny, my)
    s["by_out"][0] = ch["up_face"] * (sum_last + ch["up_inner"] * sum_first)
    s["by_out"][1] = ch["down_face"] * (sum_first + ch["down_inner"] * sum_last)

    def send_ends(axis, me, count, out, gather):
        for step in range(1, count):
            peer = lax.rem(me + step, count)
            pltpu.make_async_remote_copy(
                src_ref=out.at[jnp.where(peer > me, 0, 1)],
                dst_ref=gather.buf.at[me],
                send_sem=gather.send.at[step - 1],
                recv_sem=gather.recv.at[me],
                device_id={axis: peer},
                device_id_type=MESH,
            ).start()

    send_ends("gy", my, ny, s["by_out"], side_y)
    s["by"][my] = jnp.zeros((NZ, NX), jnp.float32)

    def load(name):
        return lambda i: s[name][i]

    chain_base(NY, load("fy"), load("y_rho"), load("y_inv"), put("yb"))
    s["yb"][0] = jnp.zeros((NZ, NX), jnp.float32)
    s["yb"][NY - 1] = jnp.zeros((NZ, NX), jnp.float32)
    first = ch["aa"] * sum_first + ch["cc"] * sum_last
    final = ch["cc"] * sum_first + ch["bb"] * sum_last
    side_y.wait_recv()
    for q in range(ny):
        b = s["by"][q]
        first = first + to_f[q] * b
        final = final + to_l[q] * b
    for y in range(NY):
        s["u2"][pl.ds(y * 8, 8), :] = s["yb"][y] + s["y_p"][y] * first + s["y_q"][y] * final

    ch, to_f, to_l = reduced_weights(info_z, s["iz"], nz, mz)
    sum_first, sum_last = 0.0, 0.0
    for z in range(NZ):
        u = jnp.concatenate([s["u2"][pl.ds(tile * 64 + z, 8, stride=8), :] for tile in range(NY // 8)], axis=0)
        f = u - 0.5 * s["lz"][z]
        s["fz"][z] = f
        sum_first = sum_first + s["z_p"][z] * f
        sum_last = sum_last + s["z_q"][z] * f
    s["bz_out"][0] = ch["up_face"] * (sum_last + ch["up_inner"] * sum_first)
    s["bz_out"][1] = ch["down_face"] * (sum_first + ch["down_inner"] * sum_last)
    send_ends("gz", mz, nz, s["bz_out"], side_z)
    s["bz"][mz] = jnp.zeros((NY, NX), jnp.float32)
    chain_base(NZ, load("fz"), load("z_rho"), load("z_inv"), put("zb"))
    s["zb"][0] = jnp.zeros((NY, NX), jnp.float32)
    s["zb"][NZ - 1] = jnp.zeros((NY, NX), jnp.float32)
    first = ch["aa"] * sum_first + ch["cc"] * sum_last
    final = ch["cc"] * sum_first + ch["bb"] * sum_last
    side_z.wait_recv()
    for q in range(nz):
        b = s["bz"][q]
        first = first + to_f[q] * b
        final = final + to_l[q] * b
    for z in range(NZ):
        out_ref[pl.ds(z * NY, NY), :] = s["zb"][z] + s["z_p"][z] * first + s["z_q"][z] * final

    for group in (halo_y, halo_z, info_x, info_y, info_z, side_x, side_y):
        group.wait_send()
    for step in range(1, nz):
        pltpu.make_async_remote_copy(
            src_ref=s["bz_out"].at[0], dst_ref=s["bz"].at[0], send_sem=side_z.send.at[step - 1],
            recv_sem=side_z.recv.at[0], device_id={"gz": lax.rem(mz + step, nz)}, device_id_type=MESH,
        ).wait_send()


def scratch(counts):
    nx, ny, nz = counts
    f32 = jnp.float32
    ycells, zcells = (NY, NZ, NX), (NZ, NY, NX)
    vmem = dict(
        tc=(2, NZ * NY, NX), ty=ycells, cy=ycells, fx=ycells, fy=ycells, ly=ycells, lz=zcells, fz=zcells,
        lzy=(NZ * NY, NX), u2=(NZ * NY, NX), eyy=ycells, ez=zcells,
        x_inv=ycells, x_p=ycells, x_q=ycells, x_keep=(7,) + ycells, x_low=(7,) + ycells, x_high=(7,) + ycells,
        y_rho=ycells, y_inv=ycells, y_p=ycells, y_q=ycells, yb=ycells,
        z_rho=zcells, z_inv=zcells, z_p=zcells, z_q=zcells, zb=zcells,
        ey=(2, 2, NZ, NX), hy=(2, 2, NZ, NX), hz=(2, 2, NY, NX),
        ix=(nx, 2, NZ, NX), bx=(nx, NZ, NX), wx=(nx, 2, NZ, NX),
        iy=(ny, 4, NZ, NX), by=(ny, NZ, NX), by_out=(2, NZ, NX),
        iz=(nz, 4, NY, NX), bz=(nz, NY, NX), bz_out=(2, NY, NX),
    )
    out = {name: pltpu.VMEM(shape, f32) for name, shape in vmem.items()}
    out["load"] = pltpu.SemaphoreType.DMA((2,))
    for name, count in (("hz", 2), ("hy", 2), ("ix", nx), ("iy", ny), ("iz", nz), ("bx", nx), ("by", ny), ("bz", nz)):
        out[name + "_s"] = pltpu.SemaphoreType.DMA((count,))
        out[name + "_r"] = pltpu.SemaphoreType.DMA((count,))
    return out


def solution(mesh):
    counts = (mesh.shape["gx"], mesh.shape["gy"], mesh.shape["gz"])
    shapes = scratch(counts)
    names = list(shapes)

    def body(t_hbm, c_hbm, out_ref, *refs):
        kernel(counts, t_hbm, c_hbm, out_ref, dict(zip(names, refs)))

    def on_device(thermal_state, diffusion_ratio):
        rows = NZ * NY
        out = pl.pallas_call(
            body,
            out_shape=jax.ShapeDtypeStruct((rows, NX), jnp.float32),
            in_specs=[pl.BlockSpec(memory_space=pl.ANY)] * 2,
            out_specs=pl.BlockSpec(memory_space=pltpu.VMEM),
            scratch_shapes=[shapes[name] for name in names],
            compiler_params=pltpu.CompilerParams(
                collective_id=0, has_side_effects=True, vmem_limit_bytes=24 * 1024 * 1024
            ),
        )(thermal_state.reshape(rows, NX), diffusion_ratio.reshape(rows, NX))
        return out.reshape(NZ, NY, NX)

    spec = P("gz", "gy", "gx")
    return jax.shard_map(on_device, mesh=mesh, in_specs=(spec, spec), out_specs=spec, check_vma=False)
```

```python
import functools

import jax
import jax.numpy as jnp
from jax import lax
from jax.experimental import pallas as pl
from jax.experimental.pallas import tpu as pltpu
from jax.sharding import PartitionSpec as P

MESH = pl.DeviceIdType.MESH
NZ, NY, NX = 8, 32, 128
SEG = 16


def rcp(x):
    return 1.0 / x


def edge(a, b):
    return a * b * rcp(a + b)


class Gather:
    def __init__(self, axis, count, buf, send, recv):
        self.axis, self.count, self.buf, self.send, self.recv = axis, count, buf, send, recv
        self.me = lax.axis_index(axis)
        self.steps = sorted(range(1, count), key=lambda step: -min(step, count - step))

    def copy(self, slot, peer, step):
        return pltpu.make_async_remote_copy(
            src_ref=self.buf.at[slot],
            dst_ref=self.buf.at[slot],
            send_sem=self.send.at[step - 1],
            recv_sem=self.recv.at[slot],
            device_id={self.axis: peer},
            device_id_type=MESH,
        )

    def start(self):
        for step in self.steps:
            self.copy(self.me, lax.rem(self.me + step, self.count), step).start()

    def wait_recv(self):
        for step in self.steps:
            peer = lax.rem(self.me + step, self.count)
            self.copy(peer, peer, step).wait_recv()

    def wait_send(self):
        for step in self.steps:
            self.copy(self.me, lax.rem(self.me + step, self.count), step).wait_send()


class Halo:
    def __init__(self, axis, count, low, high, buf, send, recv):
        self.axis, self.count, self.buf, self.send, self.recv = axis, count, buf, send, recv
        self.me = lax.axis_index(axis)
        self.ends = (high, low)

    def copy(self, side):
        step = (1, self.count - 1)[side]
        return pltpu.make_async_remote_copy(
            src_ref=self.ends[side],
            dst_ref=self.buf.at[side],
            send_sem=self.send.at[side],
            recv_sem=self.recv.at[side],
            device_id={self.axis: lax.rem(self.me + step, self.count)},
            device_id_type=MESH,
        )

    def start(self):
        for side in range(2):
            self.copy(side).start()

    def wait_recv(self):
        for side in range(2):
            self.copy(side).wait_recv()

    def wait_send(self):
        for side in range(2):
            self.copy(side).wait_send()


def near(count, reach):
    return sorted({s % count for r in range(1, reach + 1) for s in (r, -r)} - {0})


class Relay:
    def __init__(self, axis, count, reach, sem):
        self.axis, self.count, self.sem = axis, count, sem
        self.me = lax.axis_index(axis)
        self.rounds = []
        while reach < count // 2:
            self.rounds.append(reach)
            reach *= 2

    def fire(self, at):
        if at < len(self.rounds):
            for step in (self.rounds[at], self.count - self.rounds[at]):
                pl.semaphore_signal(
                    self.sem.at[at], inc=1, device_id={self.axis: lax.rem(self.me + step, self.count)},
                    device_id_type=MESH,
                )

    def wait(self, at):
        if at < len(self.rounds):
            pl.semaphore_wait(self.sem.at[at], 2)


def tree(values):
    values = list(values)
    while len(values) > 1:
        values = [sum(values[i:i + 2]) for i in range(0, len(values), 2)]
    return values[0]


def chain_matrix(edges, grounds, store_rho, store_inv, store_p, store_q):
    last = len(edges)
    rhos, lambdas = [None] * last, [None] * (last + 1)
    from_high, from_low = edges[last - 1], edges[0]
    for k in range(last - 1):
        i = last - 2 - k
        inv = rcp(edges[i] + (grounds[i + 1] + from_high))
        rhos[i] = edges[i] * inv
        store_rho(i, rhos[i])
        store_inv(i, inv)
        from_high = rhos[i] * (grounds[i + 1] + from_high)
        i = 2 + k
        lambdas[i] = edges[i - 1] * rcp(edges[i - 1] + (grounds[i - 1] + from_low))
        from_low = lambdas[i] * (grounds[i - 1] + from_low)
    one = jnp.ones_like(edges[0])
    zero = jnp.zeros_like(one)
    store_p(0, one)
    store_p(last, zero)
    store_q(0, zero)
    store_q(last, one)
    resp_p, ground_first = one, grounds[0]
    resp_q, ground_last = one, grounds[last]
    for k in range(last - 1):
        resp_p = rhos[k] * resp_p
        store_p(k + 1, resp_p)
        ground_first = ground_first + resp_p * grounds[k + 1]
        i = last - k
        resp_q = lambdas[i] * resp_q
        store_q(i - 1, resp_q)
        ground_last = ground_last + resp_q * grounds[i - 1]
    return ground_first, ground_last, edges[0] * resp_q


def chain_base(length, side, rho, inv, store):
    sums = [None] * length
    total = side(length - 2)
    sums[length - 2] = total
    for i in range(length - 3, 0, -1):
        total = side(i) + rho(i) * total
        sums[i] = total
    value = inv(0) * sums[1]
    store(1, value)
    for i in range(1, length - 2):
        value = rho(i) * value + inv(i) * sums[i + 1]
        store(i + 1, value)


def device_chain(count, me, ground_first, ground_last, inner, face):
    up_inner, up_face, gf = [None] * count, [None] * (count + 1), [None] * count
    gf[0] = ground_first[0]
    for q in range(count):
        up_inner[q] = inner[q] * rcp(inner[q] + gf[q])
        if q < count - 1:
            behind = ground_last[q] + up_inner[q] * gf[q]
            up_face[q + 1] = face[q + 1] * rcp(face[q + 1] + behind)
            gf[q + 1] = ground_first[q + 1] + up_face[q + 1] * behind
    down_inner, down_face, gl = [None] * count, [None] * (count + 1), [None] * count
    gl[count - 1] = ground_last[count - 1]
    for q in range(count - 1, -1, -1):
        down_inner[q] = inner[q] * rcp(inner[q] + gl[q])
        if q > 0:
            behind = ground_first[q] + down_inner[q] * gl[q]
            down_face[q] = face[q] * rcp(face[q] + behind)
            gl[q - 1] = ground_last[q - 1] + down_face[q] * behind
    zero = jnp.zeros_like(gf[0])

    def own(values):
        out = zero
        for q in range(count):
            if values[q] is not None:
                out = jnp.where(me == q, values[q], out)
        return out

    own_f, own_l, own_i = own(gf), own(gl), own(inner)
    scale = rcp(own_f * (own_l + own_i) + own_i * own_l)
    aa, bb, cc = (own_l + own_i) * scale, (own_f + own_i) * scale, own_i * scale
    from_low_f, from_low_l = [zero] * count, [zero] * count
    via_low = [zero] * count
    carry = zero
    for q in range(count - 2, -1, -1):
        via_low[q] = jnp.where(me == q + 1, 1.0, carry)
        from_low_l[q] = via_low[q] * up_face[q + 1]
        from_low_f[q] = from_low_l[q] * up_inner[q]
        carry = from_low_f[q]
    from_high_f, from_high_l = [zero] * count, [zero] * count
    via_high = [zero] * count
    carry = zero
    for q in range(1, count):
        via_high[q] = jnp.where(me == q - 1, 1.0, carry)
        from_high_f[q] = via_high[q] * down_face[q]
        from_high_l[q] = from_high_f[q] * down_inner[q]
        carry = from_high_l[q]
    return dict(
        aa=aa, bb=bb, cc=cc,
        low_f=from_low_f, low_l=from_low_l, high_f=from_high_f, high_l=from_high_l,
        via_low=via_low, via_high=via_high,
        up_inner=own(up_inner), up_face=own(up_face[1:]), down_inner=own(down_inner), down_face=own(down_face[:count]),
    )


def end_weights(ch, count, me, q):
    here = jnp.where(me == q, 1.0, 0.0)
    lf, ll = ch["low_f"][q] + here, ch["low_l"][q]
    hf, hl = ch["high_f"][q], ch["high_l"][q] + here
    return (
        ch["aa"] * lf + ch["cc"] * hf, ch["aa"] * ll + ch["cc"] * hl,
        ch["cc"] * lf + ch["bb"] * hf, ch["cc"] * ll + ch["bb"] * hl,
    )


def kernel(counts, t_hbm, c_hbm, out_ref, s):
    nx, ny, nz = counts
    mx, my, mz = lax.axis_index("gx"), lax.axis_index("gy"), lax.axis_index("gz")
    tc = s["tc"]
    load_c = pltpu.make_async_copy(c_hbm, tc.at[1], s["load"].at[1])
    load_t = pltpu.make_async_copy(t_hbm, tc.at[0], s["load"].at[0])
    load_c.start()
    load_t.start()
    barrier = pltpu.get_barrier_semaphore()
    greeted = 0
    for axis, me, count, reach in (("gx", mx, nx, 2), ("gz", mz, nz, 1), ("gy", my, ny, 1)):
        for step in reversed(near(count, reach)):
            pl.semaphore_signal(
                barrier, inc=1, device_id={axis: lax.rem(me + step, count)}, device_id_type=MESH
            )
            greeted += 1

    def put(name):
        def store(i, value):
            s[name][i] = value
        return store

    def load(name):
        return lambda i: s[name][i]

    halo_z = Halo("gz", nz, tc.at[:, pl.ds(0, NY)], tc.at[:, pl.ds((NZ - 1) * NY, NY)], s["hz"], s["hz_s"], s["hz_r"])
    halo_y = Halo("gy", ny, s["ey"].at[0], s["ey"].at[1], s["hy"], s["hy_s"], s["hy_r"])
    info_x = Gather("gx", nx, s["ix"], s["ix_s"], s["ix_r"])
    info_y = Gather("gy", ny, s["iy"], s["iy_s"], s["iy_r"])
    info_z = Gather("gz", nz, s["iz"], s["iz_s"], s["iz_r"])
    side_x = Gather("gx", nx, s["bx"], s["bx_s"], s["bx_r"])
    side_y = Gather("gy", ny, s["by"], s["by_s"], s["by_r"])
    side_z = Gather("gz", nz, s["bz"], s["bz_s"], s["bz_r"])
    relay_x = Relay("gx", nx, 2, s["rx"])
    relay_y = Relay("gy", ny, 1, s["ry"])
    relay_z = Relay("gz", nz, 1, s["rz"])

    load_c.wait()
    load_t.wait()
    for side, y in ((0, 0), (1, NY - 1)):
        for k in range(2):
            s["ey"][side, k] = tc[k, pl.ds(y, NZ, stride=NY), :]
    if greeted:
        pl.semaphore_wait(barrier, greeted)
    halo_z.start()
    halo_y.start()
    relay_x.fire(0)
    relay_y.fire(0)
    relay_z.fire(0)

    for half in range(2):
        for k, name in ((0, "tx"), (1, "cx")):
            block = jnp.concatenate(
                [tc[k, pl.ds(y, NZ, stride=NY), :] for y in range(16 * half, 16 * half + 16)], axis=0
            )
            s["ty" if k == 0 else "cy"][pl.ds(16 * half, 16)] = block.reshape(16, NZ, NX)
            s[name][half, pl.ds(0, NX), :] = block.T
            s[name][half, pl.ds(NX, 8), :] = jnp.ones((8, NX), jnp.float32)

    def cells(name, j):
        return jnp.stack([s[name][half, pl.ds(j, 8, stride=SEG), :] for half in range(2)])

    def put_cells(name, j, value):
        for half in range(2):
            s[name][half, pl.ds(j, 8, stride=SEG), :] = value[half]

    c = [cells("cx", j) for j in range(SEG + 1)]
    t = [cells("tx", j) for j in range(SEG + 1)]
    seg = lax.broadcasted_iota(jnp.int32, (2, 8, NX), 1)
    edges = [edge(c[j], c[j + 1]) for j in range(SEG)]
    flux = [2.0 * edges[j] * (t[j + 1] - t[j]) for j in range(SEG)]
    gap, gap_flux = edges.pop(), jnp.where(seg == 7, 0.0, flux[SEG - 1])
    flux[SEG - 1] = gap_flux
    before = pltpu.roll(gap_flux, 1, 1)
    for j in range(SEG):
        put_cells("fx", j, t[j] + 0.5 * (flux[j] - before))
        before = flux[j]
    one = jnp.ones_like(gap)
    g_first, g_last, inner = chain_matrix(
        edges, [one] * SEG, put("sx_rho"), put("sx_inv"), put("sx_p"), put("sx_q")
    )
    for k, value in enumerate((g_first, g_last, inner, gap)):
        s["l2"][k] = value.reshape(16, NX)

    def row(name, k, at):
        return s[name][k, pl.ds(at, 2, stride=8), :]

    grounds, edges = [], []
    for at in range(8):
        grounds += [row("l2", 0, at), row("l2", 1, at)]
        edges += [row("l2", 2, at)] + ([row("l2", 3, at)] if at < 7 else [])

    def put_node(name):
        def store(i, value):
            s[name][i % 2, pl.ds(i // 2, 2, stride=8), :] = value
        return store

    g_first, g_last, inner = chain_matrix(
        edges, grounds, put("l2_rho"), put("l2_inv"), put_node("l2_p"), put_node("l2_q")
    )
    for name, level in (("xp", "l2_p"), ("xq", "l2_q")):
        at_first, at_last = s[level][0].reshape(2, 8, NX), s[level][1].reshape(2, 8, NX)
        for j in range(SEG):
            put_cells(name, j, s["sx_p"][j] * at_first + s["sx_q"][j] * at_last)
    for k, name, x in ((0, "tx", 0), (1, "tx", NX - 1), (2, "cx", 0), (3, "cx", NX - 1)):
        for half in range(2):
            s["ix"][mx, pl.ds(half * 8 + k, 1), :] = s[name][half, pl.ds(x, 1), :]
    for k, value in ((4, g_first), (5, g_last), (6, inner)):
        s["ix"][mx, pl.ds(k, 2, stride=8), :] = value
    relay_x.wait(0)
    info_x.start()
    relay_y.wait(0)
    relay_y.fire(1)

    tz = [tc[0, pl.ds(z * NY, NY), :] for z in range(NZ)]
    cz = [tc[1, pl.ds(z * NY, NY), :] for z in range(NZ)]
    edges_z = [edge(cz[z], cz[z + 1]) for z in range(NZ - 1)]
    before = None
    for z in range(NZ):
        after = 2.0 * edges_z[z] * (tz[z + 1] - tz[z]) if z < NZ - 1 else None
        lap = after if before is None else (-before if after is None else after - before)
        before = after
        s["lz"][z] = lap
        if 0 < z < NZ - 1:
            for tile in range(NY // 8):
                s["lzy"][pl.ds(tile * 64 + z, 8, stride=8), :] = lap[tile * 8:tile * 8 + 8]
    edges_y = [edge(s["cy"][y], s["cy"][y + 1]) for y in range(NY - 1)]
    before = None
    for y in range(NY):
        after = 2.0 * edges_y[y] * (s["ty"][y + 1] - s["ty"][y]) if y < NY - 1 else None
        lap = after if before is None else (-before if after is None else after - before)
        before = after
        s["ly"][y] = lap
    one = jnp.ones((NZ, NX), jnp.float32)
    ends_y = chain_matrix(edges_y, [one] * NY, put("y_rho"), put("y_inv"), put("y_p"), put("y_q"))
    for k in range(3):
        s["iy"][my, k] = ends_y[k]
    one = jnp.ones((NY, NX), jnp.float32)
    ends_z = chain_matrix(edges_z, [one] * NZ, put("z_rho"), put("z_inv"), put("z_p"), put("z_q"))
    for k in range(3):
        s["iz"][mz, k] = ends_z[k]

    halo_y.wait_recv()
    halo_z.wait_recv()
    for side in range(2):
        at_wall = mz == (0, nz - 1)[side]
        z = (0, NZ - 1)[side]
        t_end, c_end = tc[0, pl.ds(z * NY, NY), :], tc[1, pl.ds(z * NY, NY), :]
        face = jnp.where(at_wall, c_end, edge(s["hz"][side, 1], c_end))
        beyond = jnp.where(at_wall, 0.0, s["hz"][side, 0])
        lap = s["lz"][z] + 2.0 * face * (beyond - t_end)
        s["lz"][z] = lap
        for tile in range(NY // 8):
            s["lzy"][pl.ds(tile * 64 + z, 8, stride=8), :] = lap[tile * 8:tile * 8 + 8]
        s["fz"][side] = face
    for side in range(2):
        at_wall = my == (0, ny - 1)[side]
        y = (0, NY - 1)[side]
        t_end, c_end = s["ty"][y], s["cy"][y]
        face = jnp.where(at_wall, c_end, edge(s["hy"][side, 1], c_end))
        beyond = jnp.where(at_wall, 0.0, s["hy"][side, 0])
        s["ly"][y] = s["ly"][y] + 2.0 * face * (beyond - t_end)
        s["fy"][side] = face

    for half in range(2):
        lap = s["ly"][pl.ds(16 * half, 16)].reshape(NX, NX) + s["lzy"][pl.ds(NX * half, NX), :]
        f = s["fx"][half] + lap.T
        s["fx"][half] = f
        for k, name in ((0, "xp"), (1, "xq")):
            part = jnp.sum((s[name][half] * f).reshape(16, 8, NX), axis=0)
            s["bx"][mx, pl.ds(2 * k + half, 1), :] = jnp.sum(part, axis=0, keepdims=True)
    side_x.start()

    relay_y.wait(1)
    relay_z.wait(0)
    face_low, face_high = s["fy"][0], s["fy"][1]
    s["iy"][my, 0] = s["iy"][my, 0] + jnp.where(my == 0, face_low, 0.0)
    s["iy"][my, 1] = s["iy"][my, 1] + jnp.where(my == ny - 1, face_high, 0.0)
    s["iy"][my, 3] = face_low
    info_y.start()
    face_low, face_high = s["fz"][0], s["fz"][1]
    s["iz"][mz, 0] = s["iz"][mz, 0] + jnp.where(mz == 0, face_low, 0.0)
    s["iz"][mz, 1] = s["iz"][mz, 1] + jnp.where(mz == nz - 1, face_high, 0.0)
    s["iz"][mz, 3] = face_low
    info_z.start()

    f = [cells("fx", j) for j in range(SEG)]
    s["l2_b"][0] = (f[0] + tree([s["sx_p"][j] * f[j] for j in range(1, SEG - 1)])).reshape(16, NX)
    s["l2_b"][1] = (f[SEG - 1] + tree([s["sx_q"][j] * f[j] for j in range(1, SEG - 1)])).reshape(16, NX)
    chain_base(16, lambda i: row("l2_b", i % 2, i // 2), load("l2_rho"), load("l2_inv"), put_node("l2_v"))
    nothing = jnp.zeros((2, NX), jnp.float32)
    put_node("l2_v")(0, nothing)
    put_node("l2_v")(15, nothing)
    at_first, at_last = s["l2_v"][0].reshape(2, 8, NX), s["l2_v"][1].reshape(2, 8, NX)

    def put_base(j, value):
        put_cells("xb", j, value + s["sx_p"][j] * at_first + s["sx_q"][j] * at_last)

    chain_base(SEG, lambda j: f[j], load("sx_rho"), load("sx_inv"), put_base)
    put_cells("xb", 0, at_first)
    put_cells("xb", SEG - 1, at_last)

    info_x.wait_recv()
    parts = [[row("ix", q, k) for k in range(7)] for q in range(nx)]
    faces = [None] * nx
    add_f, add_l = [None] * nx, [None] * nx
    gf, gl = [p[4] for p in parts], [p[5] for p in parts]
    add_f[0] = -parts[0][2] * parts[0][0]
    gf[0] = gf[0] + parts[0][2]
    add_l[nx - 1] = -parts[nx - 1][3] * parts[nx - 1][1]
    gl[nx - 1] = gl[nx - 1] + parts[nx - 1][3]
    for q in range(1, nx):
        faces[q] = edge(parts[q - 1][3], parts[q][2])
        flow = faces[q] * (parts[q][0] - parts[q - 1][1])
        add_f[q] = -flow
        add_l[q - 1] = flow
    ch = device_chain(nx, mx, gf, gl, [p[6] for p in parts], faces)
    const_f, const_l = 0.0, 0.0
    for q in range(nx):
        ff, fl, lf, ll = end_weights(ch, nx, mx, q)
        const_f = const_f + ff * add_f[q] + fl * add_l[q]
        const_l = const_l + lf * add_f[q] + ll * add_l[q]
        s["wx"][q, 0, pl.ds(0, 2), :] = ff
        s["wx"][q, 0, pl.ds(2, 2), :] = fl
        s["wx"][q, 1, pl.ds(0, 2), :] = lf
        s["wx"][q, 1, pl.ds(2, 2), :] = ll
    side_x.wait_recv()
    b = [s["bx"][q, pl.ds(0, 4), :] for q in range(nx)]
    first = tree([s["wx"][q, 0, pl.ds(0, 4), :] * b[q] for q in range(nx)])
    final = tree([s["wx"][q, 1, pl.ds(0, 4), :] * b[q] for q in range(nx)])
    first = first[0:2] + first[2:4] + const_f
    final = final[0:2] + final[2:4] + const_l

    sums_first, sums_last = [], []
    for half in range(2):
        u = s["xb"][half] + s["xp"][half] * first[half:half + 1] + s["xq"][half] * final[half:half + 1]
        rows = pl.ds(16 * half, 16)
        f = u.T.reshape(16, NZ, NX) - 0.5 * s["ly"][rows]
        s["fyy"][rows] = f
        sums_first += list(s["y_p"][rows] * f)
        sums_last += list(s["y_q"][rows] * f)
    s["by"][my, 0] = tree(sums_first)
    s["by"][my, 1] = tree(sums_last)
    side_y.start()

    chain_base(NY, load("fyy"), load("y_rho"), load("y_inv"), put("yb"))
    s["yb"][0] = jnp.zeros((NZ, NX), jnp.float32)
    s["yb"][NY - 1] = jnp.zeros((NZ, NX), jnp.float32)
    info_y.wait_recv()
    ch = device_chain(ny, my, *[[s["iy"][q, k] for q in range(ny)] for k in range(4)])
    for q in range(ny):
        for k, weight in enumerate(end_weights(ch, ny, my, q)):
            s["wy"][q, k] = weight
    info_z.wait_recv()
    ch = device_chain(nz, mz, *[[s["iz"][q, k] for q in range(nz)] for k in range(4)])
    for q in range(nz):
        s["wz"][q, 0] = ch["aa"] * ch["via_low"][q] + ch["cc"] * ch["via_high"][q]
        s["wz"][q, 1] = ch["cc"] * ch["via_low"][q] + ch["bb"] * ch["via_high"][q]
    for k, name in enumerate(("aa", "bb", "cc", "up_inner", "up_face", "down_inner", "down_face")):
        s["vz"][k] = ch[name]
    s["bz"][mz] = jnp.zeros((NY, NX), jnp.float32)
    side_y.wait_recv()
    first = tree([s["wy"][q, k] * s["by"][q, k] for q in range(ny) for k in range(2)])
    final = tree([s["wy"][q, 2 + k] * s["by"][q, k] for q in range(ny) for k in range(2)])
    for y in range(NY):
        s["u2"][pl.ds(y * 8, 8), :] = s["yb"][y] + s["y_p"][y] * first + s["y_q"][y] * final

    sums_first, sums_last = [], []
    for z in range(NZ):
        u = jnp.concatenate([s["u2"][pl.ds(tile * 64 + z, 8, stride=8), :] for tile in range(NY // 8)], axis=0)
        f = u - 0.5 * s["lz"][z]
        s["fzz"][z] = f
        sums_first.append(s["z_p"][z] * f)
        sums_last.append(s["z_q"][z] * f)
    sum_first, sum_last = tree(sums_first), tree(sums_last)
    s["bz_out"][0] = s["vz"][4] * (sum_last + s["vz"][3] * sum_first)
    s["bz_out"][1] = s["vz"][6] * (sum_first + s["vz"][5] * sum_last)

    def send_z(step):
        peer = lax.rem(mz + step, nz)
        return pltpu.make_async_remote_copy(
            src_ref=s["bz_out"].at[jnp.where(peer > mz, 0, 1)], dst_ref=s["bz"].at[mz],
            send_sem=side_z.send.at[step - 1], recv_sem=side_z.recv.at[mz],
            device_id={"gz": peer}, device_id_type=MESH,
        )

    for step in side_z.steps:
        send_z(step).start()
    first = s["vz"][0] * sum_first + s["vz"][2] * sum_last
    final = s["vz"][2] * sum_first + s["vz"][1] * sum_last
    chain_base(NZ, load("fzz"), load("z_rho"), load("z_inv"), put("zb"))
    s["zb"][0] = jnp.zeros((NY, NX), jnp.float32)
    s["zb"][NZ - 1] = jnp.zeros((NY, NX), jnp.float32)
    for group in (halo_y, halo_z, info_x, info_y, info_z, side_x, side_y):
        group.wait_send()
    side_z.wait_recv()
    first = first + tree([s["wz"][q, 0] * s["bz"][q] for q in range(nz)])
    final = final + tree([s["wz"][q, 1] * s["bz"][q] for q in range(nz)])
    for z in range(NZ):
        out_ref[pl.ds(z * NY, NY), :] = s["zb"][z] + s["z_p"][z] * first + s["z_q"][z] * final
    for step in side_z.steps:
        send_z(step).wait_send()


def scratch(counts):
    nx, ny, nz = counts
    f32 = jnp.float32
    ycells, zcells, xcells = (NY, NZ, NX), (NZ, NY, NX), (2, NX, NX)
    segs, nodes = (SEG, 2, 8, NX), (2, 16, NX)
    vmem = dict(
        tc=(2, NZ * NY, NX), ty=ycells, cy=ycells, tx=(2, NX + 8, NX), cx=(2, NX + 8, NX), fx=xcells, xp=xcells,
        xq=xcells, xb=xcells, sx_rho=segs, sx_inv=segs, sx_p=segs, sx_q=segs, l2=(4, 16, NX), l2_rho=(16, 2, NX),
        l2_inv=(16, 2, NX), l2_p=nodes, l2_q=nodes, l2_b=nodes, l2_v=nodes,
        fyy=ycells, ly=ycells, lz=zcells, fzz=zcells, lzy=(NZ * NY, NX), u2=(NZ * NY, NX),
        y_rho=ycells, y_inv=ycells, y_p=ycells, y_q=ycells, yb=ycells,
        z_rho=zcells, z_inv=zcells, z_p=zcells, z_q=zcells, zb=zcells,
        ey=(2, 2, NZ, NX), hy=(2, 2, NZ, NX), hz=(2, 2, NY, NX), fy=(2, NZ, NX), fz=(2, NY, NX),
        ix=(nx, 16, NX), bx=(nx, 8, NX), wx=(nx, 2, 8, NX),
        iy=(ny, 4, NZ, NX), by=(ny, 2, NZ, NX), wy=(ny, 4, NZ, NX),
        iz=(nz, 4, NY, NX), bz=(nz, NY, NX), bz_out=(2, NY, NX), wz=(nz, 2, NY, NX), vz=(7, NY, NX),
    )
    out = {name: pltpu.VMEM(shape, f32) for name, shape in vmem.items()}
    out["load"] = pltpu.SemaphoreType.DMA((2,))
    for name, count in (("hz", 2), ("hy", 2), ("ix", nx), ("iy", ny), ("iz", nz), ("bx", nx), ("by", ny), ("bz", nz)):
        out[name + "_s"] = pltpu.SemaphoreType.DMA((count,))
        out[name + "_r"] = pltpu.SemaphoreType.DMA((count,))
    for name in ("rx", "ry", "rz"):
        out[name] = pltpu.SemaphoreType.REGULAR((2,))
    return out


def solution(mesh):
    counts = (mesh.shape["gx"], mesh.shape["gy"], mesh.shape["gz"])
    shapes = scratch(counts)
    names = list(shapes)

    def body(t_hbm, c_hbm, out_ref, *refs):
        kernel(counts, t_hbm, c_hbm, out_ref, dict(zip(names, refs)))

    def on_device(thermal_state, diffusion_ratio):
        rows = NZ * NY
        out = pl.pallas_call(
            body,
            out_shape=jax.ShapeDtypeStruct((rows, NX), jnp.float32),
            in_specs=[pl.BlockSpec(memory_space=pltpu.HBM)] * 2,
            out_specs=pl.BlockSpec(memory_space=pltpu.VMEM),
            scratch_shapes=[shapes[name] for name in names],
            compiler_params=pltpu.CompilerParams(
                collective_id=0, has_side_effects=True, vmem_limit_bytes=24 * 1024 * 1024
            ),
        )(*[pltpu.with_memory_space_constraint(v.reshape(rows, NX), pltpu.HBM) for v in (thermal_state, diffusion_ratio)])
        return out.reshape(NZ, NY, NX)

    spec = P("gz", "gy", "gx")
    return jax.shard_map(on_device, mesh=mesh, in_specs=(spec, spec), out_specs=spec, check_vma=False)
```

```python
import functools

import jax
import jax.numpy as jnp
from jax import lax
from jax.experimental import pallas as pl
from jax.experimental.pallas import tpu as pltpu
from jax.sharding import PartitionSpec as P

MESH = pl.DeviceIdType.MESH
NZ, NY, NX = 8, 32, 128
SEG = 16


def rcp(x):
    return 1.0 / x


def edge(a, b):
    return a * b * rcp(a + b)


class Gather:
    def __init__(self, axis, count, buf, send, recv):
        self.axis, self.count, self.buf, self.send, self.recv = axis, count, buf, send, recv
        self.me = lax.axis_index(axis)
        self.steps = sorted(range(1, count), key=lambda step: -min(step, count - step))

    def start(self, source=None):
        for step in self.steps:
            peer = lax.rem(self.me + step, self.count)
            pltpu.make_async_remote_copy(
                src_ref=self.buf.at[self.me] if source is None else source(peer),
                dst_ref=self.buf.at[self.me],
                send_sem=self.send,
                recv_sem=self.recv,
                device_id={self.axis: peer},
                device_id_type=MESH,
            ).start()

    def all_peers(self):
        slots = self.buf.at[pl.ds(0, self.count - 1)]
        return pltpu.make_async_remote_copy(
            src_ref=slots, dst_ref=slots, send_sem=self.send, recv_sem=self.recv,
            device_id={self.axis: lax.rem(self.me + 1, self.count)}, device_id_type=MESH,
        )

    def wait_recv(self):
        if self.count > 1:
            self.all_peers().wait_recv()

    def wait_send(self):
        if self.count > 1:
            self.all_peers().wait_send()


class Halo:
    def __init__(self, axis, count, low, high, buf, send, recv):
        self.axis, self.count, self.buf, self.send, self.recv = axis, count, buf, send, recv
        self.me = lax.axis_index(axis)
        self.ends = (high, low)

    def copy(self, side):
        return pltpu.make_async_remote_copy(
            src_ref=self.buf if side is None else self.ends[side],
            dst_ref=self.buf if side is None else self.buf.at[side],
            send_sem=self.send,
            recv_sem=self.recv,
            device_id={self.axis: lax.rem(self.me + (self.count - 1 if side else 1), self.count)},
            device_id_type=MESH,
        )

    def start(self):
        if self.count > 1:
            for side in range(2):
                self.copy(side).start()

    def wait_recv(self):
        if self.count > 1:
            self.copy(None).wait_recv()

    def wait_send(self):
        if self.count > 1:
            self.copy(None).wait_send()


def near(count, reach):
    return sorted({s % count for r in range(1, reach + 1) for s in (r, -r)} - {0}, key=lambda s: min(s, count - s))


class Relay:
    def __init__(self, axis, count, reach, sem):
        self.axis, self.count, self.sem = axis, count, sem
        self.me = lax.axis_index(axis)
        self.rounds = []
        while reach < count // 2:
            self.rounds.append(reach)
            reach *= 2

    def fire(self, at):
        if at < len(self.rounds):
            for step in (self.rounds[at], self.count - self.rounds[at]):
                pl.semaphore_signal(
                    self.sem.at[at], inc=1, device_id={self.axis: lax.rem(self.me + step, self.count)},
                    device_id_type=MESH,
                )

    def wait(self, at):
        if at < len(self.rounds):
            pl.semaphore_wait(self.sem.at[at], 2)


def tree(values):
    values = list(values)
    while len(values) > 1:
        values = [sum(values[i:i + 2]) for i in range(0, len(values), 2)]
    return values[0]


def chain_matrix(edges, grounds, store_rho, store_inv, store_p, store_q):
    last = len(edges)
    rhos, lambdas = [None] * last, [None] * (last + 1)
    from_high, from_low = edges[last - 1], edges[0]
    for k in range(last - 1):
        i = last - 2 - k
        inv = rcp(edges[i] + (grounds[i + 1] + from_high))
        rhos[i] = edges[i] * inv
        store_rho(i, rhos[i])
        store_inv(i, inv)
        from_high = rhos[i] * (grounds[i + 1] + from_high)
        i = 2 + k
        lambdas[i] = edges[i - 1] * rcp(edges[i - 1] + (grounds[i - 1] + from_low))
        from_low = lambdas[i] * (grounds[i - 1] + from_low)
    one = jnp.ones_like(edges[0])
    zero = jnp.zeros_like(one)
    store_p(0, one)
    store_p(last, zero)
    store_q(0, zero)
    store_q(last, one)
    resp_p, ground_first = one, grounds[0]
    resp_q, ground_last = one, grounds[last]
    for k in range(last - 1):
        resp_p = rhos[k] * resp_p
        store_p(k + 1, resp_p)
        ground_first = ground_first + resp_p * grounds[k + 1]
        i = last - k
        resp_q = lambdas[i] * resp_q
        store_q(i - 1, resp_q)
        ground_last = ground_last + resp_q * grounds[i - 1]
    return ground_first, ground_last, edges[0] * resp_q


def chain_base(length, side, rho, inv, store):
    sums = [None] * length
    total = side(length - 2)
    sums[length - 2] = total
    for i in range(length - 3, 0, -1):
        total = side(i) + rho(i) * total
        sums[i] = total
    value = inv(0) * sums[1]
    store(1, value)
    for i in range(1, length - 2):
        value = rho(i) * value + inv(i) * sums[i + 1]
        store(i + 1, value)


def device_chain(count, me, ground_first, ground_last, inner, face):
    up_inner, up_face, gf = [None] * count, [None] * (count + 1), [None] * count
    gf[0] = ground_first[0]
    for q in range(count):
        up_inner[q] = inner[q] * rcp(inner[q] + gf[q])
        if q < count - 1:
            behind = ground_last[q] + up_inner[q] * gf[q]
            up_face[q + 1] = face[q + 1] * rcp(face[q + 1] + behind)
            gf[q + 1] = ground_first[q + 1] + up_face[q + 1] * behind
    down_inner, down_face, gl = [None] * count, [None] * (count + 1), [None] * count
    gl[count - 1] = ground_last[count - 1]
    for q in range(count - 1, -1, -1):
        down_inner[q] = inner[q] * rcp(inner[q] + gl[q])
        if q > 0:
            behind = ground_first[q] + down_inner[q] * gl[q]
            down_face[q] = face[q] * rcp(face[q] + behind)
            gl[q - 1] = ground_last[q - 1] + down_face[q] * behind
    zero = jnp.zeros_like(gf[0])

    def own(values):
        out = zero
        for q in range(count):
            if values[q] is not None:
                out = jnp.where(me == q, values[q], out)
        return out

    own_f, own_l, own_i = own(gf), own(gl), own(inner)
    scale = rcp(own_f * (own_l + own_i) + own_i * own_l)
    aa, bb, cc = (own_l + own_i) * scale, (own_f + own_i) * scale, own_i * scale
    from_low_f, from_low_l = [zero] * count, [zero] * count
    via_low = [zero] * count
    carry = zero
    for q in range(count - 2, -1, -1):
        via_low[q] = jnp.where(me == q + 1, 1.0, carry)
        from_low_l[q] = via_low[q] * up_face[q + 1]
        from_low_f[q] = from_low_l[q] * up_inner[q]
        carry = from_low_f[q]
    from_high_f, from_high_l = [zero] * count, [zero] * count
    via_high = [zero] * count
    carry = zero
    for q in range(1, count):
        via_high[q] = jnp.where(me == q - 1, 1.0, carry)
        from_high_f[q] = via_high[q] * down_face[q]
        from_high_l[q] = from_high_f[q] * down_inner[q]
        carry = from_high_l[q]
    return dict(
        aa=aa, bb=bb, cc=cc,
        low_f=from_low_f, low_l=from_low_l, high_f=from_high_f, high_l=from_high_l,
        via_low=via_low, via_high=via_high,
        up_inner=own(up_inner), up_face=own(up_face[1:]), down_inner=own(down_inner), down_face=own(down_face[:count]),
    )


def end_weights(ch, count, me, q):
    here = jnp.where(me == q, 1.0, 0.0)
    lf, ll = ch["low_f"][q] + here, ch["low_l"][q]
    hf, hl = ch["high_f"][q], ch["high_l"][q] + here
    return (
        ch["aa"] * lf + ch["cc"] * hf, ch["aa"] * ll + ch["cc"] * hl,
        ch["cc"] * lf + ch["bb"] * hf, ch["cc"] * ll + ch["bb"] * hl,
    )


def kernel(counts, t_hbm, c_hbm, out_ref, s):
    nx, ny, nz = counts
    mx, my, mz = lax.axis_index("gx"), lax.axis_index("gy"), lax.axis_index("gz")
    tc = s["tc"]
    load_c = pltpu.make_async_copy(c_hbm, tc.at[1], s["load"].at[1])
    load_t = pltpu.make_async_copy(t_hbm, tc.at[0], s["load"].at[0])
    load_c.start()
    load_t.start()
    barrier = pltpu.get_barrier_semaphore()
    greeted = 0
    for axis, me, count, reach in (("gz", mz, nz, 1), ("gy", my, ny, 1), ("gx", mx, nx, nx // 2)):
        for step in near(count, reach):
            pl.semaphore_signal(
                barrier, inc=1, device_id={axis: lax.rem(me + step, count)}, device_id_type=MESH
            )
            greeted += 1

    def put(name):
        def store(i, value):
            s[name][i] = value
        return store

    def load(name):
        return lambda i: s[name][i]

    halo_z = Halo("gz", nz, tc.at[:, pl.ds(0, NY)], tc.at[:, pl.ds((NZ - 1) * NY, NY)], s["hz"], s["hz_s"], s["hz_r"])
    halo_y = Halo("gy", ny, s["ey"].at[0], s["ey"].at[1], s["hy"], s["hy_s"], s["hy_r"])
    info_x = Gather("gx", nx, s["ix"], s["ix_s"], s["ix_r"])
    info_y = Gather("gy", ny, s["iy"], s["iy_s"], s["iy_r"])
    info_z = Gather("gz", nz, s["iz"], s["iz_s"], s["iz_r"])
    side_x = Gather("gx", nx, s["bx"], s["bx_s"], s["bx_r"])
    side_y = Gather("gy", ny, s["by"], s["by_s"], s["by_r"])
    side_z = Gather("gz", nz, s["bz"], s["bz_s"], s["bz_r"])
    relay_y = Relay("gy", ny, 1, s["ry"])
    relay_z = Relay("gz", nz, 1, s["rz"])

    load_c.wait()
    load_t.wait()
    for side, y in ((0, 0), (1, NY - 1)):
        for k in range(2):
            s["ey"][side, k] = tc[k, pl.ds(y, NZ, stride=NY), :]
    if greeted:
        pl.semaphore_wait(barrier, greeted)
    halo_z.start()
    halo_y.start()
    relay_y.fire(0)
    relay_z.fire(0)

    for half in range(2):
        for k, name in ((0, "tx"), (1, "cx")):
            block = jnp.concatenate(
                [tc[k, pl.ds(y, NZ, stride=NY), :] for y in range(16 * half, 16 * half + 16)], axis=0
            )
            s["ty" if k == 0 else "cy"][pl.ds(16 * half, 16)] = block.reshape(16, NZ, NX)
            s[name][half, pl.ds(0, NX), :] = block.T
            s[name][half, pl.ds(NX, 8), :] = jnp.ones((8, NX), jnp.float32)

    def cells(name, j):
        return jnp.stack([s[name][half, pl.ds(j, 8, stride=SEG), :] for half in range(2)])

    def put_cells(name, j, value):
        for half in range(2):
            s[name][half, pl.ds(j, 8, stride=SEG), :] = value[half]

    c = [cells("cx", j) for j in range(SEG + 1)]
    t = [cells("tx", j) for j in range(SEG + 1)]
    seg = lax.broadcasted_iota(jnp.int32, (2, 8, NX), 1)
    edges = [edge(c[j], c[j + 1]) for j in range(SEG)]
    flux = [2.0 * edges[j] * (t[j + 1] - t[j]) for j in range(SEG)]
    gap, gap_flux = edges.pop(), jnp.where(seg == 7, 0.0, flux[SEG - 1])
    flux[SEG - 1] = gap_flux
    before = pltpu.roll(gap_flux, 1, 1)
    for j in range(SEG):
        put_cells("fx", j, t[j] + 0.5 * (flux[j] - before))
        before = flux[j]
    one = jnp.ones_like(gap)
    g_first, g_last, inner = chain_matrix(
        edges, [one] * SEG, put("sx_rho"), put("sx_inv"), put("sx_p"), put("sx_q")
    )
    for k, value in enumerate((g_first, g_last, inner, gap)):
        s["l2"][k] = value.reshape(16, NX)

    def row(name, k, at):
        return s[name][k, pl.ds(at, 2, stride=8), :]

    grounds, edges = [], []
    for at in range(8):
        grounds += [row("l2", 0, at), row("l2", 1, at)]
        edges += [row("l2", 2, at)] + ([row("l2", 3, at)] if at < 7 else [])

    def put_node(name):
        def store(i, value):
            s[name][i % 2, pl.ds(i // 2, 2, stride=8), :] = value
        return store

    g_first, g_last, inner = chain_matrix(
        edges, grounds, put("l2_rho"), put("l2_inv"), put_node("l2_p"), put_node("l2_q")
    )
    for name, level in (("xp", "l2_p"), ("xq", "l2_q")):
        at_first, at_last = s[level][0].reshape(2, 8, NX), s[level][1].reshape(2, 8, NX)
        for j in range(SEG):
            put_cells(name, j, s["sx_p"][j] * at_first + s["sx_q"][j] * at_last)
    for k, name, x in ((0, "tx", 0), (1, "tx", NX - 1), (2, "cx", 0), (3, "cx", NX - 1)):
        for half in range(2):
            s["ix"][mx, pl.ds(half * 8 + k, 1), :] = s[name][half, pl.ds(x, 1), :]
    for k, value in ((4, g_first), (5, g_last), (6, inner)):
        s["ix"][mx, pl.ds(k, 2, stride=8), :] = value
    info_x.start()

    tz = [tc[0, pl.ds(z * NY, NY), :] for z in range(NZ)]
    cz = [tc[1, pl.ds(z * NY, NY), :] for z in range(NZ)]
    edges_z = [edge(cz[z], cz[z + 1]) for z in range(NZ - 1)]
    before = None
    for z in range(NZ):
        after = 2.0 * edges_z[z] * (tz[z + 1] - tz[z]) if z < NZ - 1 else None
        lap = after if before is None else (-before if after is None else after - before)
        before = after
        s["lz"][z] = lap
        if 0 < z < NZ - 1:
            for tile in range(NY // 8):
                s["lzy"][pl.ds(tile * 64 + z, 8, stride=8), :] = lap[tile * 8:tile * 8 + 8]
    edges_y = [edge(s["cy"][y], s["cy"][y + 1]) for y in range(NY - 1)]
    before = None
    for y in range(NY):
        after = 2.0 * edges_y[y] * (s["ty"][y + 1] - s["ty"][y]) if y < NY - 1 else None
        lap = after if before is None else (-before if after is None else after - before)
        before = after
        s["ly"][y] = lap
    one = jnp.ones((NZ, NX), jnp.float32)
    ends_y = chain_matrix(edges_y, [one] * NY, put("y_rho"), put("y_inv"), put("y_p"), put("y_q"))
    for k in range(3):
        s["iy"][my, k] = ends_y[k]
    one = jnp.ones((NY, NX), jnp.float32)
    ends_z = chain_matrix(edges_z, [one] * NZ, put("z_rho"), put("z_inv"), put("z_p"), put("z_q"))
    for k in range(3):
        s["iz"][mz, k] = ends_z[k]

    halo_y.wait_recv()
    halo_z.wait_recv()
    for side in range(2):
        at_wall = mz == (0, nz - 1)[side]
        z = (0, NZ - 1)[side]
        t_end, c_end = tc[0, pl.ds(z * NY, NY), :], tc[1, pl.ds(z * NY, NY), :]
        face = jnp.where(at_wall, c_end, edge(s["hz"][side, 1], c_end))
        beyond = jnp.where(at_wall, 0.0, s["hz"][side, 0])
        lap = s["lz"][z] + 2.0 * face * (beyond - t_end)
        s["lz"][z] = lap
        for tile in range(NY // 8):
            s["lzy"][pl.ds(tile * 64 + z, 8, stride=8), :] = lap[tile * 8:tile * 8 + 8]
        s["fz"][side] = face
    for side in range(2):
        at_wall = my == (0, ny - 1)[side]
        y = (0, NY - 1)[side]
        t_end, c_end = s["ty"][y], s["cy"][y]
        face = jnp.where(at_wall, c_end, edge(s["hy"][side, 1], c_end))
        beyond = jnp.where(at_wall, 0.0, s["hy"][side, 0])
        s["ly"][y] = s["ly"][y] + 2.0 * face * (beyond - t_end)
        s["fy"][side] = face

    for half in range(2):
        lap = s["ly"][pl.ds(16 * half, 16)].reshape(NX, NX) + s["lzy"][pl.ds(NX * half, NX), :]
        f = s["fx"][half] + lap.T
        s["fx"][half] = f
        for k, name in ((0, "xp"), (1, "xq")):
            part = jnp.sum((s[name][half] * f).reshape(16, 8, NX), axis=0)
            s["bx"][mx, pl.ds(2 * k + half, 1), :] = jnp.sum(part, axis=0, keepdims=True)
    side_x.start()

    relay_y.wait(0)
    relay_y.fire(1)
    relay_z.wait(0)
    face_low, face_high = s["fz"][0], s["fz"][1]
    s["iz"][mz, 0] = s["iz"][mz, 0] + jnp.where(mz == 0, face_low, 0.0)
    s["iz"][mz, 1] = s["iz"][mz, 1] + jnp.where(mz == nz - 1, face_high, 0.0)
    s["iz"][mz, 3] = face_low
    info_z.start()

    f = [cells("fx", j) for j in range(SEG)]
    s["l2_b"][0] = (f[0] + tree([s["sx_p"][j] * f[j] for j in range(1, SEG - 1)])).reshape(16, NX)
    s["l2_b"][1] = (f[SEG - 1] + tree([s["sx_q"][j] * f[j] for j in range(1, SEG - 1)])).reshape(16, NX)
    chain_base(16, lambda i: row("l2_b", i % 2, i // 2), load("l2_rho"), load("l2_inv"), put_node("l2_v"))
    nothing = jnp.zeros((2, NX), jnp.float32)
    put_node("l2_v")(0, nothing)
    put_node("l2_v")(15, nothing)
    at_first, at_last = s["l2_v"][0].reshape(2, 8, NX), s["l2_v"][1].reshape(2, 8, NX)

    def put_base(j, value):
        put_cells("xb", j, value + s["sx_p"][j] * at_first + s["sx_q"][j] * at_last)

    chain_base(SEG, lambda j: f[j], load("sx_rho"), load("sx_inv"), put_base)
    put_cells("xb", 0, at_first)
    put_cells("xb", SEG - 1, at_last)

    relay_y.wait(1)
    face_low, face_high = s["fy"][0], s["fy"][1]
    s["iy"][my, 0] = s["iy"][my, 0] + jnp.where(my == 0, face_low, 0.0)
    s["iy"][my, 1] = s["iy"][my, 1] + jnp.where(my == ny - 1, face_high, 0.0)
    s["iy"][my, 3] = face_low
    info_y.start()

    info_x.wait_recv()
    parts = [[row("ix", q, k) for k in range(7)] for q in range(nx)]
    faces = [None] * nx
    add_f, add_l = [None] * nx, [None] * nx
    gf, gl = [p[4] for p in parts], [p[5] for p in parts]
    add_f[0] = -parts[0][2] * parts[0][0]
    gf[0] = gf[0] + parts[0][2]
    add_l[nx - 1] = -parts[nx - 1][3] * parts[nx - 1][1]
    gl[nx - 1] = gl[nx - 1] + parts[nx - 1][3]
    for q in range(1, nx):
        faces[q] = edge(parts[q - 1][3], parts[q][2])
        flow = faces[q] * (parts[q][0] - parts[q - 1][1])
        add_f[q] = -flow
        add_l[q - 1] = flow
    ch = device_chain(nx, mx, gf, gl, [p[6] for p in parts], faces)
    const_f, const_l = 0.0, 0.0
    for q in range(nx):
        ff, fl, lf, ll = end_weights(ch, nx, mx, q)
        const_f = const_f + ff * add_f[q] + fl * add_l[q]
        const_l = const_l + lf * add_f[q] + ll * add_l[q]
        s["wx"][q, 0, pl.ds(0, 2), :] = ff
        s["wx"][q, 0, pl.ds(2, 2), :] = fl
        s["wx"][q, 1, pl.ds(0, 2), :] = lf
        s["wx"][q, 1, pl.ds(2, 2), :] = ll
    side_x.wait_recv()
    b = [s["bx"][q, pl.ds(0, 4), :] for q in range(nx)]
    first = tree([s["wx"][q, 0, pl.ds(0, 4), :] * b[q] for q in range(nx)])
    final = tree([s["wx"][q, 1, pl.ds(0, 4), :] * b[q] for q in range(nx)])
    first = first[0:2] + first[2:4] + const_f
    final = final[0:2] + final[2:4] + const_l

    sums_first, sums_last = [], []
    for half in range(2):
        u = s["xb"][half] + s["xp"][half] * first[half:half + 1] + s["xq"][half] * final[half:half + 1]
        rows = pl.ds(16 * half, 16)
        f = u.T.reshape(16, NZ, NX) - 0.5 * s["ly"][rows]
        s["fyy"][rows] = f
        sums_first += list(s["y_p"][rows] * f)
        sums_last += list(s["y_q"][rows] * f)
    s["by"][my, 0] = tree(sums_first)
    s["by"][my, 1] = tree(sums_last)
    side_y.start()

    chain_base(NY, load("fyy"), load("y_rho"), load("y_inv"), put("yb"))
    s["yb"][0] = jnp.zeros((NZ, NX), jnp.float32)
    s["yb"][NY - 1] = jnp.zeros((NZ, NX), jnp.float32)
    info_y.wait_recv()
    ch = device_chain(ny, my, *[[s["iy"][q, k] for q in range(ny)] for k in range(4)])
    for q in range(ny):
        for k, weight in enumerate(end_weights(ch, ny, my, q)):
            s["wy"][q, k] = weight
    info_z.wait_recv()
    ch = device_chain(nz, mz, *[[s["iz"][q, k] for q in range(nz)] for k in range(4)])
    for q in range(nz):
        s["wz"][q, 0] = ch["aa"] * ch["via_low"][q] + ch["cc"] * ch["via_high"][q]
        s["wz"][q, 1] = ch["cc"] * ch["via_low"][q] + ch["bb"] * ch["via_high"][q]
    for k, name in enumerate(("aa", "bb", "cc", "up_inner", "up_face", "down_inner", "down_face")):
        s["vz"][k] = ch[name]
    s["bz"][mz] = jnp.zeros((NY, NX), jnp.float32)
    side_y.wait_recv()
    first = tree([s["wy"][q, k] * s["by"][q, k] for q in range(ny) for k in range(2)])
    final = tree([s["wy"][q, 2 + k] * s["by"][q, k] for q in range(ny) for k in range(2)])
    for y in range(NY):
        s["u2"][pl.ds(y * 8, 8), :] = s["yb"][y] + s["y_p"][y] * first + s["y_q"][y] * final

    sums_first, sums_last = [], []
    for z in range(NZ):
        u = jnp.concatenate([s["u2"][pl.ds(tile * 64 + z, 8, stride=8), :] for tile in range(NY // 8)], axis=0)
        f = u - 0.5 * s["lz"][z]
        s["fzz"][z] = f
        sums_first.append(s["z_p"][z] * f)
        sums_last.append(s["z_q"][z] * f)
    sum_first, sum_last = tree(sums_first), tree(sums_last)
    s["bz_out"][0] = s["vz"][4] * (sum_last + s["vz"][3] * sum_first)
    s["bz_out"][1] = s["vz"][6] * (sum_first + s["vz"][5] * sum_last)

    side_z.start(lambda peer: s["bz_out"].at[jnp.where(peer > mz, 0, 1)])
    first = s["vz"][0] * sum_first + s["vz"][2] * sum_last
    final = s["vz"][2] * sum_first + s["vz"][1] * sum_last
    chain_base(NZ, load("fzz"), load("z_rho"), load("z_inv"), put("zb"))
    s["zb"][0] = jnp.zeros((NY, NX), jnp.float32)
    s["zb"][NZ - 1] = jnp.zeros((NY, NX), jnp.float32)
    for group in (halo_y, halo_z, info_x, info_y, info_z, side_x, side_y):
        group.wait_send()
    side_z.wait_recv()
    first = first + tree([s["wz"][q, 0] * s["bz"][q] for q in range(nz)])
    final = final + tree([s["wz"][q, 1] * s["bz"][q] for q in range(nz)])
    for z in range(NZ):
        out_ref[pl.ds(z * NY, NY), :] = s["zb"][z] + s["z_p"][z] * first + s["z_q"][z] * final
    side_z.wait_send()


def scratch(counts):
    nx, ny, nz = counts
    f32 = jnp.float32
    ycells, zcells, xcells = (NY, NZ, NX), (NZ, NY, NX), (2, NX, NX)
    segs, nodes = (SEG, 2, 8, NX), (2, 16, NX)
    vmem = dict(
        tc=(2, NZ * NY, NX), ty=ycells, cy=ycells, tx=(2, NX + 8, NX), cx=(2, NX + 8, NX), fx=xcells, xp=xcells,
        xq=xcells, xb=xcells, sx_rho=segs, sx_inv=segs, sx_p=segs, sx_q=segs, l2=(4, 16, NX), l2_rho=(16, 2, NX),
        l2_inv=(16, 2, NX), l2_p=nodes, l2_q=nodes, l2_b=nodes, l2_v=nodes,
        fyy=ycells, ly=ycells, lz=zcells, fzz=zcells, lzy=(NZ * NY, NX), u2=(NZ * NY, NX),
        y_rho=ycells, y_inv=ycells, y_p=ycells, y_q=ycells, yb=ycells,
        z_rho=zcells, z_inv=zcells, z_p=zcells, z_q=zcells, zb=zcells,
        ey=(2, 2, NZ, NX), hy=(2, 2, NZ, NX), hz=(2, 2, NY, NX), fy=(2, NZ, NX), fz=(2, NY, NX),
        ix=(nx, 16, NX), bx=(nx, 8, NX), wx=(nx, 2, 8, NX),
        iy=(ny, 4, NZ, NX), by=(ny, 2, NZ, NX), wy=(ny, 4, NZ, NX),
        iz=(nz, 4, NY, NX), bz=(nz, NY, NX), bz_out=(2, NY, NX), wz=(nz, 2, NY, NX), vz=(7, NY, NX),
    )
    out = {name: pltpu.VMEM(shape, f32) for name, shape in vmem.items()}
    out["load"] = pltpu.SemaphoreType.DMA((2,))
    for name in ("hz", "hy", "ix", "iy", "iz", "bx", "by", "bz"):
        out[name + "_s"] = pltpu.SemaphoreType.DMA
        out[name + "_r"] = pltpu.SemaphoreType.DMA
    for name in ("ry", "rz"):
        out[name] = pltpu.SemaphoreType.REGULAR((2,))
    return out


def solution(mesh):
    counts = (mesh.shape["gx"], mesh.shape["gy"], mesh.shape["gz"])
    shapes = scratch(counts)
    names = list(shapes)

    def body(t_hbm, c_hbm, out_ref, *refs):
        kernel(counts, t_hbm, c_hbm, out_ref, dict(zip(names, refs)))

    def on_device(thermal_state, diffusion_ratio):
        rows = NZ * NY
        out = pl.pallas_call(
            body,
            out_shape=jax.ShapeDtypeStruct((rows, NX), jnp.float32),
            in_specs=[pl.BlockSpec(memory_space=pltpu.HBM)] * 2,
            out_specs=pl.BlockSpec(memory_space=pltpu.VMEM),
            scratch_shapes=[shapes[name] for name in names],
            compiler_params=pltpu.CompilerParams(
                collective_id=0, has_side_effects=True, vmem_limit_bytes=24 * 1024 * 1024
            ),
        )(*[pltpu.with_memory_space_constraint(v.reshape(rows, NX), pltpu.HBM) for v in (thermal_state, diffusion_ratio)])
        return out.reshape(NZ, NY, NX)

    spec = P("gz", "gy", "gx")
    return jax.shard_map(on_device, mesh=mesh, in_specs=(spec, spec), out_specs=spec, check_vma=False)
```
